512 devices in a mesh: seq: 32 (over z, x_hi, core), head: 16 (over y, x_lo).
Axes of the slice: x: 4 (x_hi: 2, x_lo: 2; x = x_hi * 2 + x_lo), y: 8, z: 8, core: 2. Of those that a mesh axis runs over, the one named last changes fastest.
Arguments:
- q_payload: bfloat16 [4096, 6144], P(('seq', 'head')), may hold values from -5 to 5
- k_payload: bfloat16 [4096, 6144], P(('seq', 'head')), may hold values from -4 to 4
- v_payload: bfloat16 [4096, 6144], P(('seq', 'head')), may hold values from -5 to 5
- exponents: int32 [3, 4096, 48], P(None, ('seq', 'head')), may hold values from -1 to 1
- lengths: int32 [4], replicated, may hold values from 1 to 3072, as said below
Outputs:
- attended: bfloat16 [4096, 6144], P(('seq', 'head'))
The draws below stay inside these ranges and needn't reach their ends.
Inputs may be any that keep to these rules, and one draw needn't show every extreme that they name: `lengths`: 4 counts of at least 1 that sum to 4096; the largest is exactly 3072.
All inputs are finite; a program needn't handle non-finite values.
Results may differ from the reference program's by a relative error of at most 0.0045.
Values may be sent and summed in bfloat16 or wider, within the bound.
No kernel may reach another device: no remote copies, remote signals or barrier semaphores. Data moves between devices by JAX's collectives and lax.ppermute only.
A program may use at most 64 MiB of HBM per device.

```python
import math
import jax
import jax.numpy as jnp
from jax import lax

HEADS = 48
HEAD_DIM = 128
CLIPS = 4
D = 6144
TOKENS = 4096


def draw_k_payload(key, part):
    key = jax.random.fold_in(key, 11)
    values = jnp.clip(jax.random.normal(key, (TOKENS, HEADS * HEAD_DIM)), -4.0, 4.0)
    return values.astype(jnp.bfloat16)


def draw_q_payload(key, part):
    key = jax.random.fold_in(key, 23)
    values = jnp.clip(jax.random.normal(key, (TOKENS, HEADS * HEAD_DIM)), -4.0, 4.0)
    return values.astype(jnp.bfloat16)


def draw_lengths(key, part):
    key = jax.random.fold_in(key, 37)
    cut_key, place_key = jax.random.split(key)
    largest = 3 * TOKENS // CLIPS
    remain = TOKENS - largest
    order = jax.random.permutation(cut_key, remain - 1).astype(jnp.int32) + 1
    cuts = jnp.sort(order[:CLIPS - 2])
    bounds = jnp.concatenate([jnp.zeros((1,), jnp.int32), cuts, jnp.full((1,), remain, jnp.int32)])
    pieces = (bounds[1:] - bounds[:-1]).astype(jnp.int32)
    where_big = jax.random.randint(place_key, (), 0, CLIPS).astype(jnp.int32)
    slots = jnp.arange(CLIPS, dtype=jnp.int32)
    source = jnp.clip(jnp.where(slots < where_big, slots, slots - 1), 0, CLIPS - 2)
    values = jnp.where(slots == where_big, jnp.int32(largest), jnp.take(pieces, source))
    return values.astype(jnp.int32)


def touch_ends(array, key, least, top_value):
    shape = array.shape
    spot = [jax.random.randint(jax.random.fold_in(key, axis), (), 0, shape[axis]) for axis in range(len(shape))]
    array = array.at[tuple(spot)].set(least)
    longest = shape.index(max(shape))
    spot[longest] = (spot[longest] + 1) % shape[longest]
    return array.at[tuple(spot)].set(top_value)


def block_scale(rng, shape, cuts, least, high):
    factor_of, own = 1.0, jax.random.fold_in(rng, 6)
    for position, parts in cuts:
        draws = jnp.exp(jax.random.uniform(jax.random.fold_in(own, position), (parts,), jnp.float32, least / len(cuts), high / len(cuts)))
        factor_of = factor_of * jnp.repeat(draws, shape[position] // parts).reshape([-1 if axis == position else 1 for axis in range(len(shape))])
    return factor_of


def bell_draw(stream_key, extent, width, most, shards=(), held_as=jnp.bfloat16):
    entries = width * jax.random.normal(stream_key, extent, jnp.float32)
    if shards:
        entries = entries * block_scale(stream_key, extent, shards, -0.22, 0.18)
    return jnp.clip(entries, -most, most).astype(held_as)


def setup_inputs(seed: int = 0) -> dict:
    arg_keys = jax.random.split(jax.random.key(seed), 6)
    q_payload = draw_q_payload(jax.random.fold_in(arg_keys[5], 71), 0)
    k_payload = draw_k_payload(jax.random.fold_in(arg_keys[5], 71), 0)
    v_payload = bell_draw(arg_keys[2], (TOKENS, D), 1.0, 5.0, ((0, 512),))
    exponents = touch_ends(jax.random.randint(arg_keys[3], (3, TOKENS, HEADS), -1, 2), jax.random.fold_in(arg_keys[3], 1), -1, 1).astype(jnp.int32)
    lengths = draw_lengths(jax.random.fold_in(arg_keys[5], 71), 0)
    return dict(q_payload=q_payload, k_payload=k_payload, v_payload=v_payload, exponents=exponents, lengths=lengths)


def dequantize(payload, exps):
    total_rows = payload.shape[0]
    scaling = jnp.exp2(exps.astype(jnp.float32))
    shaped = payload.astype(jnp.float32).reshape(total_rows, HEADS, HEAD_DIM)
    return (shaped * scaling[:, :, None]).astype(jnp.bfloat16)

def clip_index(lengths, positions):
    clip_ends = jnp.cumsum(lengths).astype(jnp.int32)
    return lax.optimization_barrier(jnp.sum((clip_ends[None, :] <= positions[:, None]).astype(jnp.int32), axis=1))

def reference(q_payload, k_payload, v_payload, exponents, lengths):
    query = dequantize(q_payload, exponents[0])
    keyset = dequantize(k_payload, exponents[1])
    valset = dequantize(v_payload, exponents[2])
    clips = clip_index(lengths, jnp.arange(TOKENS, dtype=jnp.int32))
    block_rows = math.gcd(TOKENS, 512)
    inverse = 1.0 / math.sqrt(HEAD_DIM)

    def one_head(index):
        q_head = lax.dynamic_index_in_dim(query, index, 1, keepdims=False)
        k_head = lax.dynamic_index_in_dim(keyset, index, 1, keepdims=False)
        v_head = lax.dynamic_index_in_dim(valset, index, 1, keepdims=False)
        q_blocks = q_head.reshape(TOKENS // block_rows, block_rows, HEAD_DIM)
        c_blocks = clips.reshape(TOKENS // block_rows, block_rows)

        def one_block(pair):
            q_block, c_block = pair
            scores = jnp.dot(q_block, k_head.T, preferred_element_type=jnp.float32) * inverse
            keep = c_block[:, None] == clips[None, :]
            scores = jnp.where(keep, scores, -1e+30)
            top = lax.optimization_barrier(jnp.max(scores, axis=1, keepdims=True))
            weights = jnp.where(keep, jnp.exp(scores - top), 0.0)
            total = lax.optimization_barrier(jnp.sum(weights, axis=1, keepdims=True))
            numer = jnp.dot(weights.astype(jnp.bfloat16), v_head, preferred_element_type=jnp.float32)
            return (numer / total).astype(jnp.bfloat16)
        return lax.map(one_block, (q_blocks, c_blocks)).reshape(TOKENS, HEAD_DIM)
    heads_out = lax.map(one_head, jnp.arange(HEADS, dtype=jnp.int32))
    return jnp.transpose(heads_out, (1, 0, 2)).reshape(TOKENS, HEADS * HEAD_DIM)
```

```python
import functools
import math

import jax
import jax.numpy as jnp
from jax import lax
from jax.experimental import pallas as pl
from jax.experimental.pallas import tpu as pltpu
from jax.sharding import Mesh
from jax.sharding import PartitionSpec as P

AXES = ("z", "xh", "core", "y", "xl")
SIZES = (8, 2, 2, 8, 2)
SLOTS = 64
HEADS = 48
HEAD = 128
ROWS = 8
OWN = SLOTS * ROWS
X = ("xh", "xl")


def pack_kernel(q_ref, k_ref, v_ref, e_ref, out_ref):
    scale = jnp.exp2(e_ref[...].astype(jnp.float32))
    for place, ref in enumerate((k_ref, v_ref, q_ref)):
        kind = (1, 2, 0)[place]
        for head in range(HEADS):
            part = ref[:, head * HEAD : (head + 1) * HEAD].astype(jnp.float32)
            out_ref[head, place * ROWS : (place + 1) * ROWS, :] = (
                part * scale[kind, :, head : head + 1]
            ).astype(jnp.bfloat16)
    out_ref[HEADS:, :, :] = jnp.zeros((SLOTS - HEADS, 3 * ROWS, HEAD), jnp.bfloat16)


def clip_of(length_ref, token):
    end = jnp.int32(0)
    clip = jnp.zeros_like(token)
    for i in range(4):
        end = end + length_ref[i]
        clip = clip + (end <= token).astype(jnp.int32)
    return clip


def token_of(row, xh, core, xl):
    z = row // 64
    y = (row // 8) % 8
    return z * 512 + xh * 256 + core * 128 + y * 16 + xl * 8 + row % 8


QB = 128


def attend_kernel(length_ref, q_ref, near_ref, far_ref, out_ref, s_ref):
    xh, xl, core = lax.axis_index("xh"), lax.axis_index("xl"), lax.axis_index("core")
    factor = math.log2(math.e) / math.sqrt(HEAD)
    key_row = lax.broadcasted_iota(jnp.int32, (1, OWN), 1)
    key_clip = []
    blocks = []
    for ref, its_core in ((near_ref, core), (far_ref, 1 - core)):
        for x in range(4):
            key_clip.append(clip_of(length_ref, token_of(key_row, x // 2, its_core, x % 2)))
            blocks.append((ref, x))
    for first in range(0, OWN, QB):
        query_row = first + lax.broadcasted_iota(jnp.int32, (QB, 1), 0)
        query_clip = clip_of(length_ref, token_of(query_row, xh, core, xl))
        query = q_ref[first : first + QB, :]
        top = jnp.full((QB, HEAD), -1e30, jnp.float32)
        for i, (ref, x) in enumerate(blocks):
            scores = lax.dot_general(
                query, ref[x, 0], (((1,), (1,)), ((), ())), preferred_element_type=jnp.float32
            )
            scores = jnp.where(query_clip == key_clip[i], scores, -1e30)
            s_ref[:, i * OWN : (i + 1) * OWN] = scores
            for j in range(0, OWN, HEAD):
                top = jnp.maximum(top, scores[:, j : j + HEAD])
        top = jnp.max(top, axis=1, keepdims=True) * factor
        total = jnp.zeros((QB, HEAD), jnp.float32)
        numerator = jnp.zeros((QB, HEAD), jnp.float32)
        for i, (ref, x) in enumerate(blocks):
            weights = jnp.exp2(s_ref[:, i * OWN : (i + 1) * OWN] * factor - top)
            for j in range(0, OWN, HEAD):
                total = total + weights[:, j : j + HEAD]
            numerator = numerator + jnp.dot(
                weights.astype(jnp.bfloat16), ref[x, 1], preferred_element_type=jnp.float32
            )
        total = jnp.sum(total, axis=1, keepdims=True)
        out_ref[first : first + QB, :] = (numerator / total).astype(jnp.bfloat16)


def unpack_kernel(in_ref, out_ref):
    for head in range(HEADS):
        out_ref[:, head * HEAD : (head + 1) * HEAD] = in_ref[head]


VMEM = pl.BlockSpec(memory_space=pltpu.VMEM)
SMEM = pl.BlockSpec(memory_space=pltpu.SMEM)


def body(q_payload, k_payload, v_payload, exponents, lengths):
    packed = pl.pallas_call(
        pack_kernel,
        out_shape=jax.ShapeDtypeStruct((SLOTS, 3 * ROWS, HEAD), jnp.bfloat16),
        in_specs=[VMEM] * 4,
        out_specs=VMEM,
    )(q_payload, k_payload, v_payload, exponents)
    mine = lax.all_to_all(packed, ("z", "y"), 0, 0, tiled=True)
    keys = mine[:, :ROWS].reshape(1, OWN, HEAD)
    values = mine[:, ROWS : 2 * ROWS].reshape(1, OWN, HEAD)
    query = mine[:, 2 * ROWS :].reshape(OWN, HEAD)
    own = jnp.concatenate([keys, values], axis=0)[None]
    near = lax.all_to_all(jnp.broadcast_to(own, (4, 2, OWN, HEAD)), X, 0, 0, tiled=True)
    far = lax.ppermute(near, "core", [(0, 1), (1, 0)])
    attended = pl.pallas_call(
        attend_kernel,
        out_shape=jax.ShapeDtypeStruct((OWN, HEAD), jnp.bfloat16),
        in_specs=[SMEM, VMEM, VMEM, VMEM],
        out_specs=VMEM,
        scratch_shapes=[pltpu.VMEM((QB, 8 * OWN), jnp.float32)],
        compiler_params=pltpu.CompilerParams(vmem_limit_bytes=40 * 2**20),
    )(lengths, query, near, far)
    back = lax.all_to_all(attended.reshape(SLOTS, ROWS, HEAD), ("z", "y"), 0, 0, tiled=True)
    return pl.pallas_call(
        unpack_kernel,
        out_shape=jax.ShapeDtypeStruct((ROWS, HEADS * HEAD), jnp.bfloat16),
        in_specs=[VMEM],
        out_specs=VMEM,
    )(back)


def solution(mesh):
    fine = Mesh(mesh.devices.reshape(SIZES), AXES)
    tokens = P(AXES, None)
    return jax.shard_map(
        body,
        mesh=fine,
        in_specs=(tokens, tokens, tokens, P(None, AXES, None), P()),
        out_specs=tokens,
        check_vma=False,
    )
```

```python
import functools
import math

import jax
import jax.numpy as jnp
from jax import lax
from jax.experimental import pallas as pl
from jax.experimental.pallas import tpu as pltpu
from jax.sharding import Mesh
from jax.sharding import PartitionSpec as P

AXES = ("z", "xh", "core", "y", "xl")
SIZES = (8, 2, 2, 8, 2)
SLOTS = 64
HEADS = 48
HEAD = 128
ROWS = 8
OWN = SLOTS * ROWS
X = ("xh", "xl")


def clip_of(length_ref, token):
    end = jnp.int32(0)
    clip = jnp.zeros_like(token)
    for i in range(4):
        end = end + length_ref[i]
        clip = clip + (end <= token).astype(jnp.int32)
    return clip


def token_of(row, xh, core, xl):
    z = row // 64
    y = (row // 8) % 8
    return z * 512 + xh * 256 + core * 128 + y * 16 + xl * 8 + row % 8


QB = 256


def attend_kernel(its_core, carried, length_ref, q_ref, kv_ref, *refs):
    if carried:
        acc_ref, top_ref, sum_ref, out_ref, s_ref = refs
    else:
        acc_ref, top_ref, sum_ref, s_ref = refs
    xh, xl, core = lax.axis_index("xh"), lax.axis_index("xl"), lax.axis_index("core")
    key_core = core if its_core else 1 - core
    factor = math.log2(math.e) / math.sqrt(HEAD)
    key_row = lax.broadcasted_iota(jnp.int32, (1, OWN), 1)
    key_clip = [
        clip_of(length_ref, token_of(key_row, x // 2, key_core, x % 2)) for x in range(4)
    ]
    blocks = OWN // QB

    def rows(block):
        return slice(block * QB, (block + 1) * QB)

    def begin(block):
        query_row = block * QB + lax.broadcasted_iota(jnp.int32, (QB, 1), 0)
        query_clip = clip_of(length_ref, token_of(query_row, xh, core, xl))
        top = top_ref[rows(block), :] if carried else jnp.full((QB, HEAD), -1e30, jnp.float32)
        return q_ref[rows(block), :], query_clip, top

    def score(block, x, query, query_clip, top):
        scores = lax.dot_general(
            query, kv_ref[x, 0], (((1,), (1,)), ((), ())), preferred_element_type=jnp.float32
        )
        scores = jnp.where(query_clip == key_clip[x], scores, -1e30)
        s_ref[block % 2, :, x * OWN : (x + 1) * OWN] = scores
        for j in range(0, OWN, HEAD):
            top = jnp.maximum(top, scores[:, j : j + HEAD])
        return top

    query, query_clip, top = begin(0)
    for x in range(4):
        top = score(0, x, query, query_clip, top)
    for block in range(blocks):
        highest = jnp.max(top, axis=1, keepdims=True)
        shift = highest * factor
        if carried:
            old = jnp.exp2(top_ref[rows(block), :] * factor - shift)
            total, numerator = sum_ref[rows(block), :] * old, acc_ref[rows(block), :] * old
        else:
            total = numerator = jnp.zeros((QB, HEAD), jnp.float32)
        if block + 1 < blocks:
            query, query_clip, top = begin(block + 1)
        for x in range(4):
            if block + 1 < blocks:
                top = score(block + 1, x, query, query_clip, top)
            weights = jnp.exp2(s_ref[block % 2, :, x * OWN : (x + 1) * OWN] * factor - shift)
            for j in range(0, OWN, HEAD):
                total = total + weights[:, j : j + HEAD]
            numerator = numerator + jnp.dot(
                weights.astype(jnp.bfloat16), kv_ref[x, 1], preferred_element_type=jnp.float32
            )
        if carried:
            out_ref[rows(block), :] = (
                numerator / jnp.sum(total, axis=1, keepdims=True)
            ).astype(jnp.bfloat16)
        else:
            acc_ref[rows(block), :] = numerator
            top_ref[rows(block), :] = jnp.broadcast_to(highest, (QB, HEAD))
            sum_ref[rows(block), :] = total


VMEM = pl.BlockSpec(memory_space=pltpu.VMEM)
SMEM = pl.BlockSpec(memory_space=pltpu.SMEM)


def attend(its_core, lengths, query, kv, state=()):
    f32 = jax.ShapeDtypeStruct((OWN, HEAD), jnp.float32)
    return pl.pallas_call(
        functools.partial(attend_kernel, its_core, bool(state)),
        out_shape=jax.ShapeDtypeStruct((OWN, HEAD), jnp.bfloat16) if state else [f32] * 3,
        in_specs=[SMEM] + [VMEM] * (2 + len(state)),
        out_specs=VMEM if state else [VMEM] * 3,
        scratch_shapes=[pltpu.VMEM((2, QB, 4 * OWN), jnp.float32)],
        compiler_params=pltpu.CompilerParams(vmem_limit_bytes=32 * 2**20),
        cost_estimate=pl.CostEstimate(
            flops=4 * OWN * 4 * OWN * HEAD, bytes_accessed=2**20, transcendentals=4 * OWN * OWN
        ),
    )(lengths, query, kv, *state)


def pack(q_payload, k_payload, v_payload, exponents):
    scale = jnp.exp2(exponents.astype(jnp.float32))
    payload = jnp.stack([q_payload, k_payload, v_payload]).reshape(3, ROWS, HEADS, HEAD)
    scaled = (payload.astype(jnp.float32) * scale[:, :, :, None]).astype(jnp.bfloat16)
    packed = scaled.transpose(2, 0, 1, 3).reshape(HEADS, 3 * ROWS, HEAD)
    return jnp.pad(packed, ((0, SLOTS - HEADS), (0, 0), (0, 0)))


def body(q_payload, k_payload, v_payload, exponents, lengths):
    packed = pack(q_payload, k_payload, v_payload, exponents)
    mine = lax.all_to_all(packed, ("z", "y"), 0, 0, tiled=True)
    query = mine[:, :ROWS].reshape(OWN, HEAD)
    own = mine[:, ROWS:].reshape(1, SLOTS, 2, ROWS, HEAD).transpose(0, 2, 1, 3, 4)
    own = own.reshape(1, 2, OWN, HEAD)
    near = lax.all_to_all(jnp.broadcast_to(own, (4, 2, OWN, HEAD)), X, 0, 0, tiled=True)
    far = lax.ppermute(near, "core", [(0, 1), (1, 0)])
    state = attend(True, lengths, query, near)
    attended = attend(False, lengths, query, far, state)
    back = lax.all_to_all(attended.reshape(SLOTS, ROWS, HEAD), ("z", "y"), 0, 0, tiled=True)
    return back[:HEADS].transpose(1, 0, 2).reshape(ROWS, HEADS * HEAD)


def solution(mesh):
    fine = Mesh(mesh.devices.reshape(SIZES), AXES)
    tokens = P(AXES, None)
    return jax.shard_map(
        body,
        mesh=fine,
        in_specs=(tokens, tokens, tokens, P(None, AXES, None), P()),
        out_specs=tokens,
        check_vma=False,
    )
```

```python
import functools
import math

import jax
import jax.numpy as jnp
from jax import lax
from jax.experimental import pallas as pl
from jax.experimental.pallas import tpu as pltpu
from jax.sharding import Mesh
from jax.sharding import PartitionSpec as P

AXES = ("z", "xh", "core", "y", "xl")
SIZES = (8, 2, 2, 8, 2)
SLOTS = 64
HEADS = 48
HEAD = 128
ROWS = 8
OWN = SLOTS * ROWS
X = ("xh", "xl")


def clip_of(length_ref, token):
    end = jnp.int32(0)
    clip = jnp.zeros_like(token)
    for i in range(4):
        end = end + length_ref[i]
        clip = clip + (end <= token).astype(jnp.int32)
    return clip


def token_of(row, xh, core, xl):
    z = row // 64
    y = (row // 8) % 8
    return z * 512 + xh * 256 + core * 128 + y * 16 + xl * 8 + row % 8


QB = 256


def attend_kernel(sources, carried, final, length_ref, q_ref, *refs):
    count = len({place for place, _, _, _ in sources})
    kv_refs, refs = refs[:count], refs[count:]
    state_refs, refs = (refs[:3], refs[3:]) if carried else ((), refs)
    out_refs, s_ref = refs[:-1], refs[-1]
    xh, xl, core = lax.axis_index("xh"), lax.axis_index("xl"), lax.axis_index("core")
    factor = math.log2(math.e) / math.sqrt(HEAD)
    key_row = lax.broadcasted_iota(jnp.int32, (1, OWN), 1)
    keys, values, key_clip = [], [], []
    for place, index, hops, cores in sources:
        x = (xh * 2 + xl + 4 - hops) % 4
        its_core = core if cores == 0 else 1 - core
        key_clip.append(clip_of(length_ref, token_of(key_row, x // 2, its_core, x % 2)))
        keys.append(kv_refs[place].at[index, 0])
        values.append(kv_refs[place].at[index, 1])
    blocks, parts = OWN // QB, len(sources)

    def rows(block):
        return slice(block * QB, (block + 1) * QB)

    def begin(block):
        query_row = block * QB + lax.broadcasted_iota(jnp.int32, (QB, 1), 0)
        query_clip = clip_of(length_ref, token_of(query_row, xh, core, xl))
        if carried:
            top = state_refs[1][rows(block), :]
        else:
            top = jnp.full((QB, HEAD), -1e30, jnp.float32)
        return q_ref[rows(block), :], query_clip, top

    def score(block, part, query, query_clip, top):
        scores = lax.dot_general(
            query, keys[part][...], (((1,), (1,)), ((), ())), preferred_element_type=jnp.float32
        )
        scores = jnp.where(query_clip == key_clip[part], scores, -1e30)
        s_ref[block % 2, :, part * OWN : (part + 1) * OWN] = scores
        for j in range(0, OWN, HEAD):
            top = jnp.maximum(top, scores[:, j : j + HEAD])
        return top

    query, query_clip, top = begin(0)
    for part in range(parts):
        top = score(0, part, query, query_clip, top)
    for block in range(blocks):
        highest = jnp.max(top, axis=1, keepdims=True)
        shift = highest * factor
        if carried:
            old = jnp.exp2(state_refs[1][rows(block), :] * factor - shift)
            numerator = state_refs[0][rows(block), :] * old
            total = state_refs[2][rows(block), :] * old
        else:
            total = numerator = jnp.zeros((QB, HEAD), jnp.float32)
        if block + 1 < blocks:
            query, query_clip, top = begin(block + 1)
        for part in range(parts):
            if block + 1 < blocks:
                top = score(block + 1, part, query, query_clip, top)
            scores = s_ref[block % 2, :, part * OWN : (part + 1) * OWN]
            weights = jnp.exp2(scores * factor - shift)
            for j in range(0, OWN, HEAD):
                total = total + weights[:, j : j + HEAD]
            numerator = numerator + jnp.dot(
                weights.astype(jnp.bfloat16), values[part][...], preferred_element_type=jnp.float32
            )
        if final:
            out_refs[0][rows(block), :] = (
                numerator / jnp.sum(total, axis=1, keepdims=True)
            ).astype(jnp.bfloat16)
        else:
            out_refs[0][rows(block), :] = numerator
            out_refs[1][rows(block), :] = jnp.broadcast_to(highest, (QB, HEAD))
            out_refs[2][rows(block), :] = total


VMEM = pl.BlockSpec(memory_space=pltpu.VMEM)
SMEM = pl.BlockSpec(memory_space=pltpu.SMEM)


def attend(sources, final, lengths, query, kvs, state=()):
    f32 = jax.ShapeDtypeStruct((OWN, HEAD), jnp.float32)
    keys = len(sources) * OWN
    return pl.pallas_call(
        functools.partial(attend_kernel, sources, bool(state), final),
        out_shape=jax.ShapeDtypeStruct((OWN, HEAD), jnp.bfloat16) if final else [f32] * 3,
        in_specs=[SMEM] + [VMEM] * (1 + len(kvs) + len(state)),
        out_specs=VMEM if final else [VMEM] * 3,
        scratch_shapes=[pltpu.VMEM((2, QB, keys), jnp.float32)],
        compiler_params=pltpu.CompilerParams(vmem_limit_bytes=32 * 2**20),
        cost_estimate=pl.CostEstimate(
            flops=4 * OWN * keys * HEAD, bytes_accessed=2**20, transcendentals=OWN * keys
        ),
    )(lengths, query, *kvs, *state)


def pack(q_payload, k_payload, v_payload, exponents):
    scale = jnp.exp2(exponents.astype(jnp.float32))
    payload = jnp.stack([q_payload, k_payload, v_payload]).reshape(3, ROWS, HEADS, HEAD)
    scaled = (payload.astype(jnp.float32) * scale[:, :, :, None]).astype(jnp.bfloat16)
    packed = scaled.transpose(2, 0, 1, 3).reshape(HEADS, 3 * ROWS, HEAD)
    return jnp.pad(packed, ((0, SLOTS - HEADS), (0, 0), (0, 0)))


def body(q_payload, k_payload, v_payload, exponents, lengths):
    packed = pack(q_payload, k_payload, v_payload, exponents)
    mine = lax.all_to_all(packed, ("z", "y"), 0, 0, tiled=True)
    query = mine[:, :ROWS].reshape(OWN, HEAD)
    own = mine[:, ROWS:].reshape(1, SLOTS, 2, ROWS, HEAD).transpose(0, 2, 1, 3, 4)
    own = own.reshape(1, 2, OWN, HEAD)
    swap = [(0, 1), (1, 0)]
    hops = (1, 3, 2)
    near = [lax.ppermute(own, X, [(x, (x + hop) % 4) for x in range(4)]) for hop in hops]
    sibling = lax.ppermute(own, "core", swap)
    state = attend(((0, 0, 0, 0), (1, 0, 0, 1)), False, lengths, query, (own, sibling))
    near, state = lax.optimization_barrier((near, state))
    far = lax.ppermute(jnp.concatenate(near), "core", swap)
    places = tuple((i, 0, hop, 0) for i, hop in enumerate(hops))
    state = attend(places, False, lengths, query, near, state)
    places = tuple((0, i, hop, 1) for i, hop in enumerate(hops))
    attended = attend(places, True, lengths, query, (far,), state)
    back = lax.all_to_all(attended.reshape(SLOTS, ROWS, HEAD), ("z", "y"), 0, 0, tiled=True)
    return back[:HEADS].transpose(1, 0, 2).reshape(ROWS, HEADS * HEAD)


def solution(mesh):
    fine = Mesh(mesh.devices.reshape(SIZES), AXES)
    tokens = P(AXES, None)
    return jax.shard_map(
        body,
        mesh=fine,
        in_specs=(tokens, tokens, tokens, P(None, AXES, None), P()),
        out_specs=tokens,
        check_vma=False,
    )
```

```python
import functools
import math

import jax
import jax.numpy as jnp
import numpy as np
from jax import lax
from jax.experimental import pallas as pl
from jax.experimental.pallas import tpu as pltpu
from jax.sharding import Mesh
from jax.sharding import PartitionSpec as P

SIZES = (8, 2, 2, 8, 2)
SLOTS = 64
HEADS = 48
HEAD = 128
ROWS = 8
OWN = SLOTS * ROWS
FIRST_Z, FIRST_Y = 5, 4
X_ORDER = [2, 3, 0, 1]
PLACES = np.arange(512).reshape(SIZES)
BY_HEAD = np.roll(PLACES, (-FIRST_Z, -FIRST_Y), (0, 3)).transpose(1, 2, 4, 0, 3).reshape(8, SLOTS)
BY_X = PLACES.transpose(0, 2, 3, 1, 4).reshape(128, 4)[:, X_ORDER]
BY_CORE = PLACES.transpose(0, 1, 3, 4, 2).reshape(256, 2)


def place():
    index = lax.axis_index("device")
    return (index // 32) % 2, index % 2, (index // 16) % 2


def clip_of(length_ref, token):
    end = jnp.int32(0)
    clip = jnp.zeros_like(token)
    for i in range(4):
        end = end + length_ref[i]
        clip = clip + (end <= token).astype(jnp.int32)
    return clip


def token_of(row, xh, core, xl):
    z = (row // 64 + FIRST_Z) % 8
    y = (row // 8 + FIRST_Y) % 8
    return z * 512 + xh * 256 + core * 128 + y * 16 + xl * 8 + row % 8


QB = 256


def attend_kernel(its_core, carried, length_ref, q_ref, kv_ref, *refs):
    if carried:
        acc_ref, top_ref, sum_ref, out_ref, s_ref = refs
    else:
        acc_ref, top_ref, sum_ref, s_ref = refs
    xh, xl, core = place()
    key_core = core if its_core else 1 - core
    factor = math.log2(math.e) / math.sqrt(HEAD)
    key_row = lax.broadcasted_iota(jnp.int32, (1, OWN), 1)
    key_clip = [
        clip_of(length_ref, token_of(key_row, x // 2, key_core, x % 2)) for x in X_ORDER
    ]
    blocks = OWN // QB

    def rows(block):
        return slice(block * QB, (block + 1) * QB)

    def begin(block):
        query_row = block * QB + lax.broadcasted_iota(jnp.int32, (QB, 1), 0)
        query_clip = clip_of(length_ref, token_of(query_row, xh, core, xl))
        top = top_ref[rows(block), :] if carried else jnp.full((QB, HEAD), -1e30, jnp.float32)
        return q_ref[rows(block), :], query_clip, top

    def score(block, x, query, query_clip, top):
        scores = lax.dot_general(
            query, kv_ref[x, 0], (((1,), (1,)), ((), ())), preferred_element_type=jnp.float32
        )
        scores = jnp.where(query_clip == key_clip[x], scores, -1e30)
        s_ref[block % 2, :, x * OWN : (x + 1) * OWN] = scores
        for j in range(0, OWN, HEAD):
            top = jnp.maximum(top, scores[:, j : j + HEAD])
        return top

    query, query_clip, top = begin(0)
    for x in range(4):
        top = score(0, x, query, query_clip, top)
    for block in range(blocks):
        highest = jnp.max(top, axis=1, keepdims=True)
        shift = highest * factor
        if carried:
            old = jnp.exp2(top_ref[rows(block), :] * factor - shift)
            total, numerator = sum_ref[rows(block), :] * old, acc_ref[rows(block), :] * old
        else:
            total = numerator = jnp.zeros((QB, HEAD), jnp.float32)
        if block + 1 < blocks:
            query, query_clip, top = begin(block + 1)
        for x in range(4):
            if block + 1 < blocks:
                top = score(block + 1, x, query, query_clip, top)
            weights = jnp.exp2(s_ref[block % 2, :, x * OWN : (x + 1) * OWN] * factor - shift)
            for j in range(0, OWN, HEAD):
                total = total + weights[:, j : j + HEAD]
            numerator = numerator + jnp.dot(
                weights.astype(jnp.bfloat16), kv_ref[x, 1], preferred_element_type=jnp.float32
            )
        if carried:
            out_ref[rows(block), :] = (
                numerator / jnp.sum(total, axis=1, keepdims=True)
            ).astype(jnp.bfloat16)
        else:
            acc_ref[rows(block), :] = numerator
            top_ref[rows(block), :] = jnp.broadcast_to(highest, (QB, HEAD))
            sum_ref[rows(block), :] = total


VMEM = pl.BlockSpec(memory_space=pltpu.VMEM)
SMEM = pl.BlockSpec(memory_space=pltpu.SMEM)


def attend(its_core, lengths, query, kv, state=()):
    f32 = jax.ShapeDtypeStruct((OWN, HEAD), jnp.float32)
    return pl.pallas_call(
        functools.partial(attend_kernel, its_core, bool(state)),
        out_shape=jax.ShapeDtypeStruct((OWN, HEAD), jnp.bfloat16) if state else [f32] * 3,
        in_specs=[SMEM] + [VMEM] * (2 + len(state)),
        out_specs=VMEM if state else [VMEM] * 3,
        scratch_shapes=[pltpu.VMEM((2, QB, 4 * OWN), jnp.float32)],
        compiler_params=pltpu.CompilerParams(vmem_limit_bytes=32 * 2**20),
        cost_estimate=pl.CostEstimate(
            flops=4 * OWN * 4 * OWN * HEAD, bytes_accessed=2**20, transcendentals=4 * OWN * OWN
        ),
    )(lengths, query, kv, *state)


def pack(q_payload, k_payload, v_payload, exponents):
    scale = jnp.exp2(exponents.astype(jnp.float32)).astype(jnp.bfloat16).reshape(3 * ROWS, HEADS)
    lane_head = jnp.arange(HEADS * HEAD) // HEAD
    spread = (jnp.arange(HEADS)[:, None] == lane_head[None, :]).astype(jnp.bfloat16)
    scale = jnp.dot(scale, spread, preferred_element_type=jnp.float32)
    payload = jnp.concatenate([q_payload, k_payload, v_payload]).astype(jnp.float32)
    packed = (payload * scale).astype(jnp.bfloat16).reshape(3 * ROWS, HEADS, HEAD)
    return jnp.pad(packed.transpose(1, 0, 2), ((0, SLOTS - HEADS), (0, 0), (0, 0)))


def exchange(array, groups):
    return lax.all_to_all(array, "device", 0, 0, axis_index_groups=groups.tolist(), tiled=True)


def body(q_payload, k_payload, v_payload, exponents, lengths):
    packed = pack(q_payload, k_payload, v_payload, exponents)
    mine = exchange(packed, BY_HEAD)
    query = mine[:, :ROWS].reshape(OWN, HEAD)
    own = mine[:, ROWS:].reshape(1, SLOTS, 2, ROWS, HEAD).transpose(0, 2, 1, 3, 4)
    own = own.reshape(1, 2, OWN, HEAD)
    near = exchange(jnp.broadcast_to(own, (4, 2, OWN, HEAD)), BY_X)
    far = lax.ppermute(near, "device", [(a, b) for a, b in BY_CORE.tolist()] + [(b, a) for a, b in BY_CORE.tolist()])
    state = attend(True, lengths, query, near)
    attended = attend(False, lengths, query, far, state)
    back = exchange(attended.reshape(SLOTS, ROWS, HEAD), BY_HEAD)
    return back[:HEADS].transpose(1, 0, 2).reshape(ROWS, HEADS * HEAD)


def solution(mesh):
    tokens = P("device", None)
    return jax.shard_map(
        body,
        mesh=Mesh(mesh.devices.reshape(-1), ("device",)),
        in_specs=(tokens, tokens, tokens, P(None, "device", None), P()),
        out_specs=tokens,
        check_vma=False,
    )
```

```python
import functools
import math

import jax
import jax.numpy as jnp
import numpy as np
from jax import lax
from jax.experimental import pallas as pl
from jax.experimental.pallas import tpu as pltpu
from jax.sharding import Mesh
from jax.sharding import PartitionSpec as P

SIZES = (8, 2, 2, 8, 2)
SLOTS = 64
HEADS = 48
HEAD = 128
ROWS = 8
OWN = SLOTS * ROWS
FIRST_Z, FIRST_Y = 5, 4
X_ORDER = [2, 0, 3, 1]
PLACES = np.arange(512).reshape(SIZES)
BY_HEAD = np.roll(PLACES, (-FIRST_Z, -FIRST_Y), (0, 3)).transpose(1, 2, 4, 3, 0).reshape(8, SLOTS)
BY_X = PLACES.transpose(0, 2, 3, 1, 4).reshape(128, 4)[:, X_ORDER]
BY_CORE = PLACES.transpose(0, 1, 3, 4, 2).reshape(256, 2)


def place():
    index = lax.axis_index("device")
    return (index // 32) % 2, index % 2, (index // 16) % 2


def clip_of(length_ref, token):
    end = jnp.int32(0)
    clip = jnp.zeros_like(token)
    for i in range(4):
        end = end + length_ref[i]
        clip = clip + (end <= token).astype(jnp.int32)
    return clip


def token_of(row, xh, core, xl):
    z = (row // 8 + FIRST_Z) % 8
    y = (row // 64 + FIRST_Y) % 8
    return z * 512 + xh * 256 + core * 128 + y * 16 + xl * 8 + row % 8


QB = 256


def attend_kernel(its_core, carried, length_ref, q_ref, kv_ref, *refs):
    if carried:
        acc_ref, top_ref, sum_ref, out_ref, s_ref = refs
    else:
        acc_ref, top_ref, sum_ref, s_ref = refs
    xh, xl, core = place()
    key_core = core if its_core else 1 - core
    factor = math.log2(math.e) / math.sqrt(HEAD)
    key_row = lax.broadcasted_iota(jnp.int32, (1, OWN), 1)
    key_clip = [
        clip_of(length_ref, token_of(key_row, x // 2, key_core, x % 2)) for x in X_ORDER
    ]
    blocks = OWN // QB

    def rows(block):
        return slice(block * QB, (block + 1) * QB)

    def begin(block):
        query_row = block * QB + lax.broadcasted_iota(jnp.int32, (QB, 1), 0)
        query_clip = clip_of(length_ref, token_of(query_row, xh, core, xl))
        top = top_ref[rows(block), :] if carried else jnp.full((QB, HEAD), -1e30, jnp.float32)
        return q_ref[rows(block), :], query_clip, top

    def score(block, x, query, query_clip, top):
        scores = lax.dot_general(
            query, kv_ref[x, 0], (((1,), (1,)), ((), ())), preferred_element_type=jnp.float32
        )
        scores = jnp.where(query_clip == key_clip[x], scores, -1e30)
        s_ref[block % 2, :, x * OWN : (x + 1) * OWN] = scores
        for j in range(0, OWN, HEAD):
            top = jnp.maximum(top, scores[:, j : j + HEAD])
        return top

    query, query_clip, top = begin(0)
    for x in range(4):
        top = score(0, x, query, query_clip, top)
    for block in range(blocks):
        highest = jnp.max(top, axis=1, keepdims=True)
        shift = highest * factor
        if carried:
            old = jnp.exp2(top_ref[rows(block), :] * factor - shift)
            total, numerator = sum_ref[rows(block), :] * old, acc_ref[rows(block), :] * old
        else:
            total = numerator = jnp.zeros((QB, HEAD), jnp.float32)
        if block + 1 < blocks:
            query, query_clip, top = begin(block + 1)
        for x in range(4):
            if block + 1 < blocks:
                top = score(block + 1, x, query, query_clip, top)
            weights = jnp.exp2(s_ref[block % 2, :, x * OWN : (x + 1) * OWN] * factor - shift)
            for j in range(0, OWN, HEAD):
                total = total + weights[:, j : j + HEAD]
            numerator = numerator + jnp.dot(
                weights.astype(jnp.bfloat16), kv_ref[x, 1], preferred_element_type=jnp.float32
            )
        if carried:
            out_ref[rows(block), :] = (
                numerator / jnp.sum(total, axis=1, keepdims=True)
            ).astype(jnp.bfloat16)
        else:
            acc_ref[rows(block), :] = numerator
            top_ref[rows(block), :] = jnp.broadcast_to(highest, (QB, HEAD))
            sum_ref[rows(block), :] = total


VMEM = pl.BlockSpec(memory_space=pltpu.VMEM)
SMEM = pl.BlockSpec(memory_space=pltpu.SMEM)


def attend(its_core, lengths, query, kv, state=()):
    f32 = jax.ShapeDtypeStruct((OWN, HEAD), jnp.float32)
    return pl.pallas_call(
        functools.partial(attend_kernel, its_core, bool(state)),
        out_shape=jax.ShapeDtypeStruct((OWN, HEAD), jnp.bfloat16) if state else [f32] * 3,
        in_specs=[SMEM] + [VMEM] * (2 + len(state)),
        out_specs=VMEM if state else [VMEM] * 3,
        scratch_shapes=[pltpu.VMEM((2, QB, 4 * OWN), jnp.float32)],
        compiler_params=pltpu.CompilerParams(vmem_limit_bytes=32 * 2**20),
        cost_estimate=pl.CostEstimate(
            flops=4 * OWN * 4 * OWN * HEAD, bytes_accessed=2**20, transcendentals=4 * OWN * OWN
        ),
    )(lengths, query, kv, *state)


def pack(q_payload, k_payload, v_payload, exponents):
    scale = jnp.exp2(exponents.astype(jnp.float32)).astype(jnp.bfloat16).reshape(3 * ROWS, HEADS)
    lane_head = jnp.arange(HEADS * HEAD) // HEAD
    spread = (jnp.arange(HEADS)[:, None] == lane_head[None, :]).astype(jnp.bfloat16)
    scale = jnp.dot(scale, spread, preferred_element_type=jnp.float32)
    payload = jnp.concatenate([q_payload, k_payload, v_payload]).astype(jnp.float32)
    packed = (payload * scale).astype(jnp.bfloat16).reshape(3 * ROWS, HEADS, HEAD)
    return jnp.pad(packed.transpose(1, 0, 2), ((0, SLOTS - HEADS), (0, 0), (0, 0)))


def exchange(array, groups):
    return lax.all_to_all(array, "device", 0, 0, axis_index_groups=groups.tolist(), tiled=True)


def body(q_payload, k_payload, v_payload, exponents, lengths):
    packed = pack(q_payload, k_payload, v_payload, exponents)
    mine = exchange(packed, BY_HEAD)
    query = mine[:, :ROWS].reshape(OWN, HEAD)
    own = mine[:, ROWS:].reshape(1, SLOTS, 2, ROWS, HEAD).transpose(0, 2, 1, 3, 4)
    own = own.reshape(1, 2, OWN, HEAD)
    near = exchange(jnp.broadcast_to(own, (4, 2, OWN, HEAD)), BY_X)
    far = lax.ppermute(near, "device", [(a, b) for a, b in BY_CORE.tolist()] + [(b, a) for a, b in BY_CORE.tolist()])
    state = attend(True, lengths, query, near)
    attended = attend(False, lengths, query, far, state)
    back = exchange(attended.reshape(SLOTS, ROWS, HEAD), BY_HEAD)
    return back[:HEADS].transpose(1, 0, 2).reshape(ROWS, HEADS * HEAD)


def solution(mesh):
    tokens = P("device", None)
    return jax.shard_map(
        body,
        mesh=Mesh(mesh.devices.reshape(-1), ("device",)),
        in_specs=(tokens, tokens, tokens, P(None, "device", None), P()),
        out_specs=tokens,
        check_vma=False,
    )
```

```python
import functools
import math

import jax
import jax.numpy as jnp
import numpy as np
from jax import lax
from jax.experimental import pallas as pl
from jax.experimental.pallas import tpu as pltpu
from jax.sharding import Mesh
from jax.sharding import PartitionSpec as P

SIZES = (8, 2, 2, 8, 2)
SLOTS = 64
HEADS = 48
HEAD = 128
ROWS = 8
OWN = SLOTS * ROWS
FIRST_Z, FIRST_Y = 5, 4
X_ORDER = [2, 0, 3, 1]
PLACES = np.arange(512).reshape(SIZES)
BY_HEAD = np.roll(PLACES, (-FIRST_Z, -FIRST_Y), (0, 3)).transpose(1, 2, 4, 3, 0).reshape(8, SLOTS)
BY_X = PLACES.transpose(0, 2, 3, 1, 4).reshape(128, 4)[:, X_ORDER]
BY_CORE = PLACES.transpose(0, 1, 3, 4, 2).reshape(256, 2)


def place():
    index = lax.axis_index("device")
    return (index // 32) % 2, index % 2, (index // 16) % 2


def clip_of(length_ref, token):
    first = length_ref[0]
    second = first + length_ref[1]
    third = second + length_ref[2]
    ends = (token >= first, token >= second, token >= third)
    return sum(end.astype(jnp.int32) for end in ends)


def token_of(row, xh, core, xl):
    z = ((row >> 3) + FIRST_Z) & 7
    y = ((row >> 6) + FIRST_Y) & 7
    return (z << 9) + (y << 4) + (row & 7) + (xh * 256 + core * 128 + xl * 8)


QB = 256


def attend_kernel(its_core, carried, length_ref, q_ref, kv_ref, *refs):
    if carried:
        acc_ref, top_ref, sum_ref, out_ref, s_ref = refs
    else:
        acc_ref, top_ref, sum_ref, s_ref = refs
    xh, xl, core = place()
    key_core = core if its_core else 1 - core
    factor = math.log2(math.e) / math.sqrt(HEAD)
    key_row = lax.broadcasted_iota(jnp.int32, (1, OWN), 1)
    key_clip = [
        clip_of(length_ref, token_of(key_row, x // 2, key_core, x % 2)) for x in X_ORDER
    ]
    blocks = OWN // QB

    def rows(block):
        return slice(block * QB, (block + 1) * QB)

    def begin(block):
        query_row = block * QB + lax.broadcasted_iota(jnp.int32, (QB, 1), 0)
        query_clip = clip_of(length_ref, token_of(query_row, xh, core, xl))
        top = top_ref[rows(block), :] if carried else jnp.full((QB, HEAD), -1e30, jnp.float32)
        return q_ref[rows(block), :], query_clip, top

    def score(block, x, query, query_clip, top):
        scores = lax.dot_general(
            query, kv_ref[x, 0], (((1,), (1,)), ((), ())), preferred_element_type=jnp.float32
        )
        scores = jnp.where(query_clip == key_clip[x], scores, -1e30)
        s_ref[block % 2, :, x * OWN : (x + 1) * OWN] = scores
        for j in range(0, OWN, HEAD):
            top = jnp.maximum(top, scores[:, j : j + HEAD])
        return top

    query, query_clip, top = begin(0)
    for x in range(4):
        top = score(0, x, query, query_clip, top)
    for block in range(blocks):
        highest = jnp.max(top, axis=1, keepdims=True)
        shift = highest * factor
        if carried:
            old = jnp.exp2(top_ref[rows(block), :] * factor - shift)
            total, numerator = sum_ref[rows(block), :] * old, acc_ref[rows(block), :] * old
        else:
            total = numerator = jnp.zeros((QB, HEAD), jnp.float32)
        if block + 1 < blocks:
            query, query_clip, top = begin(block + 1)
        for x in range(4):
            if block + 1 < blocks:
                top = score(block + 1, x, query, query_clip, top)
            weights = jnp.exp2(s_ref[block % 2, :, x * OWN : (x + 1) * OWN] * factor - shift)
            for j in range(0, OWN, HEAD):
                total = total + weights[:, j : j + HEAD]
            numerator = numerator + jnp.dot(
                weights.astype(jnp.bfloat16), kv_ref[x, 1], preferred_element_type=jnp.float32
            )
        if carried:
            out_ref[rows(block), :] = (
                numerator / jnp.sum(total, axis=1, keepdims=True)
            ).astype(jnp.bfloat16)
        else:
            acc_ref[rows(block), :] = numerator
            top_ref[rows(block), :] = jnp.broadcast_to(highest, (QB, HEAD))
            sum_ref[rows(block), :] = total


VMEM = pl.BlockSpec(memory_space=pltpu.VMEM)
SMEM = pl.BlockSpec(memory_space=pltpu.SMEM)


def attend(its_core, lengths, query, kv, state=()):
    f32 = jax.ShapeDtypeStruct((OWN, HEAD), jnp.float32)
    return pl.pallas_call(
        functools.partial(attend_kernel, its_core, bool(state)),
        out_shape=jax.ShapeDtypeStruct((OWN, HEAD), jnp.bfloat16) if state else [f32] * 3,
        in_specs=[SMEM] + [VMEM] * (2 + len(state)),
        out_specs=VMEM if state else [VMEM] * 3,
        scratch_shapes=[pltpu.VMEM((2, QB, 4 * OWN), jnp.float32)],
        compiler_params=pltpu.CompilerParams(vmem_limit_bytes=32 * 2**20),
        cost_estimate=pl.CostEstimate(
            flops=4 * OWN * 4 * OWN * HEAD, bytes_accessed=2**20, transcendentals=4 * OWN * OWN
        ),
    )(lengths, query, kv, *state)


def pack(q_payload, k_payload, v_payload, exponents):
    scale = jnp.exp2(exponents.astype(jnp.float32)).astype(jnp.bfloat16).reshape(3 * ROWS, HEADS)
    lane_head = jnp.arange(HEADS * HEAD) // HEAD
    spread = (jnp.arange(HEADS)[:, None] == lane_head[None, :]).astype(jnp.bfloat16)
    scale = jnp.dot(scale, spread, preferred_element_type=jnp.float32)
    payload = jnp.concatenate([q_payload, k_payload, v_payload]).astype(jnp.float32)
    packed = (payload * scale).astype(jnp.bfloat16).reshape(3 * ROWS, HEADS, HEAD)
    return jnp.pad(packed.transpose(1, 0, 2), ((0, SLOTS - HEADS), (0, 0), (0, 0)))


def exchange(array, groups):
    return lax.all_to_all(array, "device", 0, 0, axis_index_groups=groups.tolist(), tiled=True)


def body(q_payload, k_payload, v_payload, exponents, lengths):
    packed = pack(q_payload, k_payload, v_payload, exponents)
    mine = exchange(packed, BY_HEAD)
    query = mine[:, :ROWS].reshape(OWN, HEAD)
    own = mine[:, ROWS:].reshape(1, SLOTS, 2, ROWS, HEAD).transpose(0, 2, 1, 3, 4)
    own = own.reshape(1, 2, OWN, HEAD)
    near = exchange(jnp.broadcast_to(own, (4, 2, OWN, HEAD)), BY_X)
    far = lax.ppermute(near, "device", [(a, b) for a, b in BY_CORE.tolist()] + [(b, a) for a, b in BY_CORE.tolist()])
    state = attend(True, lengths, query, near)
    attended = attend(False, lengths, query, far, state)
    back = exchange(attended.reshape(SLOTS, ROWS, HEAD), BY_HEAD)
    return back[:HEADS].transpose(1, 0, 2).reshape(ROWS, HEADS * HEAD)


def solution(mesh):
    tokens = P("device", None)
    return jax.shard_map(
        body,
        mesh=Mesh(mesh.devices.reshape(-1), ("device",)),
        in_specs=(tokens, tokens, tokens, P(None, "device", None), P()),
        out_specs=tokens,
        check_vma=False,
    )
```

```python
import functools
import math

import jax
import jax.numpy as jnp
import numpy as np
from jax import lax
from jax.experimental import pallas as pl
from jax.experimental.pallas import tpu as pltpu
from jax.sharding import Mesh
from jax.sharding import PartitionSpec as P

SIZES = (8, 2, 2, 8, 2)
SLOTS = 64
HEADS = 48
HEAD = 128
ROWS = 8
OWN = SLOTS * ROWS
FIRST_Z, FIRST_Y = 5, 4
X_ORDER = [2, 0, 3, 1]
PLACES = np.arange(512).reshape(SIZES)
BY_HEAD = np.roll(PLACES, (-FIRST_Z, -FIRST_Y), (0, 3)).transpose(1, 2, 4, 3, 0).reshape(8, SLOTS)
BY_X = PLACES.transpose(0, 2, 3, 1, 4).reshape(128, 4)[:, X_ORDER]
BY_CORE = PLACES.transpose(0, 1, 3, 4, 2).reshape(256, 2)


def place():
    index = lax.axis_index("device")
    return (index // 32) % 2, index % 2, (index // 16) % 2


def clip_of(length_ref, token):
    first = length_ref[0]
    second = first + length_ref[1]
    third = second + length_ref[2]
    ends = (token >= first, token >= second, token >= third)
    return sum(end.astype(jnp.int32) for end in ends)


def token_of(row, xh, core, xl):
    z = ((row >> 3) + FIRST_Z) & 7
    y = ((row >> 6) + FIRST_Y) & 7
    return (z << 9) + (y << 4) + (row & 7) + (xh * 256 + core * 128 + xl * 8)


QB = 256


def attend_kernel(its_core, carried, length_ref, q_ref, kv_ref, *refs):
    if carried:
        acc_ref, top_ref, sum_ref, out_ref, s_ref = refs
    else:
        acc_ref, top_ref, sum_ref, s_ref = refs
    xh, xl, core = place()
    key_core = core if its_core else 1 - core
    factor = math.log2(math.e) / math.sqrt(HEAD)
    key_row = lax.broadcasted_iota(jnp.int32, (1, OWN), 1)
    key_clip = [
        clip_of(length_ref, token_of(key_row, x // 2, key_core, x % 2)) for x in X_ORDER
    ]
    blocks = OWN // QB

    def rows(block):
        return slice(block * QB, (block + 1) * QB)

    def begin(block):
        query_row = block * QB + lax.broadcasted_iota(jnp.int32, (QB, 1), 0)
        query_clip = clip_of(length_ref, token_of(query_row, xh, core, xl))
        top = top_ref[rows(block), :] if carried else jnp.full((QB, HEAD), -1e30, jnp.float32)
        return q_ref[rows(block), :], query_clip, top

    def score(block, x, query, query_clip, top):
        scores = lax.dot_general(
            query, kv_ref[x, 0], (((1,), (1,)), ((), ())), preferred_element_type=jnp.float32
        )
        scores = jnp.where(query_clip == key_clip[x], scores, -1e30)
        s_ref[block % 2, :, x * OWN : (x + 1) * OWN] = scores
        for j in range(0, OWN, HEAD):
            top = jnp.maximum(top, scores[:, j : j + HEAD])
        return top

    query, query_clip, top = begin(0)
    for x in range(4):
        top = score(0, x, query, query_clip, top)
    for block in range(blocks):
        highest = jnp.max(top, axis=1, keepdims=True)
        shift = highest * factor
        total = numerator = jnp.zeros((QB, HEAD), jnp.float32)
        if block + 1 < blocks:
            query, query_clip, top = begin(block + 1)
        for x in range(4):
            if block + 1 < blocks:
                top = score(block + 1, x, query, query_clip, top)
            weights = jnp.exp2(s_ref[block % 2, :, x * OWN : (x + 1) * OWN] * factor - shift)
            for j in range(0, OWN, HEAD):
                total = total + weights[:, j : j + HEAD]
            numerator = numerator + jnp.dot(
                weights.astype(jnp.bfloat16), kv_ref[x, 1], preferred_element_type=jnp.float32
            )
        if carried:
            old = jnp.exp2(top_ref[rows(block), :] * factor - shift)
            total = total + sum_ref[rows(block), :] * old
            numerator = numerator + acc_ref[rows(block), :] * old
            out_ref[rows(block), :] = (
                numerator / jnp.sum(total, axis=1, keepdims=True)
            ).astype(jnp.bfloat16)
        else:
            acc_ref[rows(block), :] = numerator
            top_ref[rows(block), :] = jnp.broadcast_to(highest, (QB, HEAD))
            sum_ref[rows(block), :] = total


VMEM = pl.BlockSpec(memory_space=pltpu.VMEM)
SMEM = pl.BlockSpec(memory_space=pltpu.SMEM)


def attend(its_core, lengths, query, kv, state=()):
    f32 = jax.ShapeDtypeStruct((OWN, HEAD), jnp.float32)
    return pl.pallas_call(
        functools.partial(attend_kernel, its_core, bool(state)),
        out_shape=jax.ShapeDtypeStruct((OWN, HEAD), jnp.bfloat16) if state else [f32] * 3,
        in_specs=[SMEM] + [VMEM] * (2 + len(state)),
        out_specs=VMEM if state else [VMEM] * 3,
        scratch_shapes=[pltpu.VMEM((2, QB, 4 * OWN), jnp.float32)],
        compiler_params=pltpu.CompilerParams(vmem_limit_bytes=32 * 2**20),
        cost_estimate=pl.CostEstimate(
            flops=4 * OWN * 4 * OWN * HEAD, bytes_accessed=2**20, transcendentals=4 * OWN * OWN
        ),
    )(lengths, query, kv, *state)


def pack(q_payload, k_payload, v_payload, exponents):
    scale = jnp.exp2(exponents.astype(jnp.float32)).astype(jnp.bfloat16).reshape(3 * ROWS, HEADS)
    lane_head = jnp.arange(SLOTS * HEAD) // HEAD
    spread = (jnp.arange(HEADS)[:, None] == lane_head[None, :]).astype(jnp.bfloat16)
    scale = jnp.dot(scale, spread, preferred_element_type=jnp.float32)
    payload = jnp.concatenate([q_payload, k_payload, v_payload]).astype(jnp.float32)
    payload = jnp.pad(payload, ((0, 0), (0, (SLOTS - HEADS) * HEAD)))
    packed = (payload * scale).astype(jnp.bfloat16).reshape(3 * ROWS, SLOTS, HEAD)
    return packed.transpose(1, 0, 2)


def exchange(array, groups):
    return lax.all_to_all(array, "device", 0, 0, axis_index_groups=groups.tolist(), tiled=True)


def body(q_payload, k_payload, v_payload, exponents, lengths):
    packed = pack(q_payload, k_payload, v_payload, exponents)
    mine = exchange(packed, BY_HEAD)
    query = mine[:, :ROWS].reshape(OWN, HEAD)
    own = mine[:, ROWS:].reshape(1, SLOTS, 2, ROWS, HEAD).transpose(0, 2, 1, 3, 4)
    own = own.reshape(1, 2, OWN, HEAD)
    near = exchange(jnp.broadcast_to(own, (4, 2, OWN, HEAD)), BY_X)
    far = lax.ppermute(near, "device", [(a, b) for a, b in BY_CORE.tolist()] + [(b, a) for a, b in BY_CORE.tolist()])
    state = attend(True, lengths, query, near)
    attended = attend(False, lengths, query, far, state)
    back = exchange(attended.reshape(SLOTS, ROWS, HEAD), BY_HEAD)
    return back[:HEADS].transpose(1, 0, 2).reshape(ROWS, HEADS * HEAD)


def solution(mesh):
    tokens = P("device", None)
    return jax.shard_map(
        body,
        mesh=Mesh(mesh.devices.reshape(-1), ("device",)),
        in_specs=(tokens, tokens, tokens, P(None, "device", None), P()),
        out_specs=tokens,
        check_vma=False,
    )
```

```python
import functools
import math

import jax
import jax.numpy as jnp
import numpy as np
from jax import lax
from jax.experimental import pallas as pl
from jax.experimental.pallas import tpu as pltpu
from jax.sharding import Mesh
from jax.sharding import PartitionSpec as P

SIZES = (8, 2, 2, 8, 2)
SLOTS = 64
HEADS = 48
HEAD = 128
ROWS = 8
OWN = SLOTS * ROWS
FIRST_Z, FIRST_Y = 5, 4
X_ORDER = [2, 0, 3, 1]
PLACES = np.arange(512).reshape(SIZES)
BY_HEAD = np.roll(PLACES, (-FIRST_Z, -FIRST_Y), (0, 3)).transpose(1, 2, 4, 3, 0).reshape(8, SLOTS)
BY_X = PLACES.transpose(0, 2, 3, 1, 4).reshape(128, 4)[:, X_ORDER]
BY_CORE = PLACES.transpose(0, 1, 3, 4, 2).reshape(256, 2)


def place():
    index = lax.axis_index("device")
    return (index // 32) % 2, index % 2, (index // 16) % 2


def clip_of(length_ref, token):
    first = length_ref[0]
    second = first + length_ref[1]
    third = second + length_ref[2]
    ends = (token >= first, token >= second, token >= third)
    return sum(end.astype(jnp.int32) for end in ends)


def token_of(row, xh, core, xl):
    z = ((row >> 3) + FIRST_Z) & 7
    y = ((row >> 6) + FIRST_Y) & 7
    return (z << 9) + (y << 4) + (row & 7) + (xh * 256 + core * 128 + xl * 8)


QB = 256


def attend_kernel(its_core, carried, length_ref, q_ref, kv_ref, *refs):
    if carried:
        acc_ref, top_ref, sum_ref, out_ref, s_ref = refs
    else:
        acc_ref, top_ref, sum_ref, s_ref = refs
    xh, xl, core = place()
    key_core = core if its_core else 1 - core
    factor = math.log2(math.e) / math.sqrt(HEAD)
    key_row = lax.broadcasted_iota(jnp.int32, (1, OWN), 1)
    key_clip = [
        clip_of(length_ref, token_of(key_row, x // 2, key_core, x % 2)) for x in X_ORDER
    ]
    blocks = OWN // QB

    def rows(block):
        return slice(block * QB, (block + 1) * QB)

    def begin(block):
        query_row = block * QB + lax.broadcasted_iota(jnp.int32, (QB, 1), 0)
        query_clip = clip_of(length_ref, token_of(query_row, xh, core, xl))
        top = top_ref[rows(block), :] if carried else jnp.full((QB, HEAD), -1e30, jnp.float32)
        return q_ref[rows(block), :], query_clip, top

    def score(block, x, query, query_clip, top):
        scores = lax.dot_general(
            query, kv_ref[x, 0], (((1,), (1,)), ((), ())), preferred_element_type=jnp.float32
        )
        scores = jnp.where(query_clip == key_clip[x], scores, -1e30)
        s_ref[block % 2, :, x * OWN : (x + 1) * OWN] = scores
        for j in range(0, OWN, HEAD):
            top = jnp.maximum(top, scores[:, j : j + HEAD])
        return top

    query, query_clip, top = begin(0)
    for x in range(4):
        top = score(0, x, query, query_clip, top)
    for block in range(blocks):
        highest = jnp.max(top, axis=1, keepdims=True)
        shift = highest * factor
        total = numerator = jnp.zeros((QB, HEAD), jnp.float32)
        if block + 1 < blocks:
            query, query_clip, top = begin(block + 1)
        for x in range(4):
            if block + 1 < blocks:
                top = score(block + 1, x, query, query_clip, top)
            weights = jnp.exp2(s_ref[block % 2, :, x * OWN : (x + 1) * OWN] * factor - shift)
            for j in range(0, OWN, HEAD):
                total = total + weights[:, j : j + HEAD]
            numerator = numerator + jnp.dot(
                weights.astype(jnp.bfloat16), kv_ref[x, 1], preferred_element_type=jnp.float32
            )
        if carried:
            old = jnp.exp2(top_ref[rows(block), :] * factor - shift)
            total = total + sum_ref[rows(block), :] * old
            numerator = numerator + acc_ref[rows(block), :] * old
            out_ref[rows(block), :] = (
                numerator / jnp.sum(total, axis=1, keepdims=True)
            ).astype(jnp.bfloat16)
        else:
            acc_ref[rows(block), :] = numerator
            top_ref[rows(block), :] = jnp.broadcast_to(highest, (QB, HEAD))
            sum_ref[rows(block), :] = total


VMEM = pl.BlockSpec(memory_space=pltpu.VMEM)
SMEM = pl.BlockSpec(memory_space=pltpu.SMEM)


def attend(its_core, lengths, query, kv, state=()):
    f32 = jax.ShapeDtypeStruct((OWN, HEAD), jnp.float32)
    return pl.pallas_call(
        functools.partial(attend_kernel, its_core, bool(state)),
        out_shape=jax.ShapeDtypeStruct((OWN, HEAD), jnp.bfloat16) if state else [f32] * 3,
        in_specs=[SMEM] + [VMEM] * (2 + len(state)),
        out_specs=VMEM if state else [VMEM] * 3,
        scratch_shapes=[pltpu.VMEM((2, QB, 4 * OWN), jnp.float32)],
        compiler_params=pltpu.CompilerParams(vmem_limit_bytes=32 * 2**20),
        cost_estimate=pl.CostEstimate(
            flops=4 * OWN * 4 * OWN * HEAD, bytes_accessed=2**20, transcendentals=4 * OWN * OWN
        ),
    )(lengths, query, kv, *state)


def pack(q_payload, k_payload, v_payload, exponents):
    scale = jnp.exp2(exponents.astype(jnp.float32)).astype(jnp.bfloat16).reshape(3 * ROWS, HEADS)
    lane_head = jnp.arange(SLOTS * HEAD) // HEAD
    spread = (jnp.arange(HEADS)[:, None] == lane_head[None, :]).astype(jnp.bfloat16)
    scale = jnp.dot(scale, spread, preferred_element_type=jnp.float32)
    payload = jnp.concatenate([q_payload, k_payload, v_payload]).astype(jnp.float32)
    payload = jnp.pad(payload, ((0, 0), (0, (SLOTS - HEADS) * HEAD)))
    packed = (payload * scale).astype(jnp.bfloat16).reshape(3 * ROWS, SLOTS, HEAD)
    return packed.transpose(1, 0, 2)


def exchange(array, groups):
    return lax.all_to_all(array, "device", 0, 0, axis_index_groups=groups.tolist(), tiled=True)


def body(q_payload, k_payload, v_payload, exponents, lengths):
    packed = pack(q_payload, k_payload, v_payload, exponents)
    mine = exchange(packed, BY_HEAD)
    query = mine[:, :ROWS].reshape(OWN, HEAD)
    own = mine[:, ROWS:].reshape(1, SLOTS, 2, ROWS, HEAD).transpose(0, 2, 1, 3, 4)
    own = own.reshape(1, 2, OWN, HEAD)
    near = exchange(jnp.concatenate([own] * 4), BY_X)
    far = lax.ppermute(near, "device", [(a, b) for a, b in BY_CORE.tolist()] + [(b, a) for a, b in BY_CORE.tolist()])
    state = attend(True, lengths, query, near)
    attended = attend(False, lengths, query, far, state)
    back = exchange(attended.reshape(SLOTS, ROWS, HEAD), BY_HEAD)
    return back[:HEADS].transpose(1, 0, 2).reshape(ROWS, HEADS * HEAD)


def solution(mesh):
    tokens = P("device", None)
    return jax.shard_map(
        body,
        mesh=Mesh(mesh.devices.reshape(-1), ("device",)),
        in_specs=(tokens, tokens, tokens, P(None, "device", None), P()),
        out_specs=tokens,
        check_vma=False,
    )
```

```python
import functools
import math

import jax
import jax.numpy as jnp
import numpy as np
from jax import lax
from jax.experimental import pallas as pl
from jax.experimental.pallas import tpu as pltpu
from jax.sharding import Mesh
from jax.sharding import PartitionSpec as P

SIZES = (8, 2, 2, 8, 2)
SLOTS = 64
HEADS = 48
HEAD = 128
ROWS = 8
OWN = SLOTS * ROWS
FIRST_Z, FIRST_Y = 5, 4
X_ORDER = [2, 1, 3, 0]
PLACES = np.arange(512).reshape(SIZES)
BY_HEAD = np.roll(PLACES, (-FIRST_Z, -FIRST_Y), (0, 3)).transpose(1, 2, 4, 3, 0).reshape(8, SLOTS)
BY_X = PLACES.transpose(0, 2, 3, 1, 4).reshape(128, 4)[:, X_ORDER]
BY_CORE = PLACES.transpose(0, 1, 3, 4, 2).reshape(256, 2)


def place():
    index = lax.axis_index("device")
    return (index // 32) % 2, index % 2, (index // 16) % 2


def clip_of(length_ref, token):
    first = length_ref[0]
    second = first + length_ref[1]
    third = second + length_ref[2]
    ends = (token >= first, token >= second, token >= third)
    return sum(end.astype(jnp.int32) for end in ends)


def token_of(row, xh, core, xl):
    z = ((row >> 3) + FIRST_Z) & 7
    y = ((row >> 6) + FIRST_Y) & 7
    return (z << 9) + (y << 4) + (row & 7) + (xh * 256 + core * 128 + xl * 8)


QB = 256


def attend_kernel(its_core, carried, length_ref, q_ref, kv_ref, *refs):
    if carried:
        acc_ref, top_ref, sum_ref, out_ref, s_ref = refs
    else:
        acc_ref, top_ref, sum_ref, s_ref = refs
    xh, xl, core = place()
    key_core = core if its_core else 1 - core
    factor = math.log2(math.e) / math.sqrt(HEAD)
    key_row = lax.broadcasted_iota(jnp.int32, (1, OWN), 1)
    key_clip = [
        clip_of(length_ref, token_of(key_row, x // 2, key_core, x % 2)) for x in X_ORDER
    ]
    blocks = OWN // QB

    def rows(block):
        return slice(block * QB, (block + 1) * QB)

    def begin(block):
        query_row = block * QB + lax.broadcasted_iota(jnp.int32, (QB, 1), 0)
        query_clip = clip_of(length_ref, token_of(query_row, xh, core, xl))
        top = top_ref[rows(block), :] if carried else jnp.full((QB, HEAD), -1e30, jnp.float32)
        return q_ref[rows(block), :], query_clip, top

    def score(block, x, query, query_clip, top):
        scores = lax.dot_general(
            query, kv_ref[x, 0], (((1,), (1,)), ((), ())), preferred_element_type=jnp.float32
        )
        scores = jnp.where(query_clip == key_clip[x], scores, -1e30)
        s_ref[block % 2, :, x * OWN : (x + 1) * OWN] = scores
        for j in range(0, OWN, HEAD):
            top = jnp.maximum(top, scores[:, j : j + HEAD])
        return top

    query, query_clip, top = begin(0)
    for x in range(4):
        top = score(0, x, query, query_clip, top)
    for block in range(blocks):
        highest = jnp.max(top, axis=1, keepdims=True)
        shift = highest * factor
        total = numerator = jnp.zeros((QB, HEAD), jnp.float32)
        if block + 1 < blocks:
            query, query_clip, top = begin(block + 1)
        for x in range(4):
            if block + 1 < blocks:
                top = score(block + 1, x, query, query_clip, top)
            weights = jnp.exp2(s_ref[block % 2, :, x * OWN : (x + 1) * OWN] * factor - shift)
            for j in range(0, OWN, HEAD):
                total = total + weights[:, j : j + HEAD]
            numerator = numerator + jnp.dot(
                weights.astype(jnp.bfloat16), kv_ref[x, 1], preferred_element_type=jnp.float32
            )
        if carried:
            old = jnp.exp2(top_ref[rows(block), :] * factor - shift)
            total = total + sum_ref[rows(block), :] * old
            numerator = numerator + acc_ref[rows(block), :] * old
            out_ref[rows(block), :] = (
                numerator / jnp.sum(total, axis=1, keepdims=True)
            ).astype(jnp.bfloat16)
        else:
            acc_ref[rows(block), :] = numerator
            top_ref[rows(block), :] = jnp.broadcast_to(highest, (QB, HEAD))
            sum_ref[rows(block), :] = total


VMEM = pl.BlockSpec(memory_space=pltpu.VMEM)
SMEM = pl.BlockSpec(memory_space=pltpu.SMEM)


def attend(its_core, lengths, query, kv, state=()):
    f32 = jax.ShapeDtypeStruct((OWN, HEAD), jnp.float32)
    return pl.pallas_call(
        functools.partial(attend_kernel, its_core, bool(state)),
        out_shape=jax.ShapeDtypeStruct((OWN, HEAD), jnp.bfloat16) if state else [f32] * 3,
        in_specs=[SMEM] + [VMEM] * (2 + len(state)),
        out_specs=VMEM if state else [VMEM] * 3,
        scratch_shapes=[pltpu.VMEM((2, QB, 4 * OWN), jnp.float32)],
        compiler_params=pltpu.CompilerParams(vmem_limit_bytes=32 * 2**20),
        cost_estimate=pl.CostEstimate(
            flops=4 * OWN * 4 * OWN * HEAD, bytes_accessed=2**20, transcendentals=4 * OWN * OWN
        ),
    )(lengths, query, kv, *state)


def pack(q_payload, k_payload, v_payload, exponents):
    scale = jnp.exp2(exponents.astype(jnp.float32)).astype(jnp.bfloat16).reshape(3 * ROWS, HEADS)
    lane_head = jnp.arange(SLOTS * HEAD) // HEAD
    spread = (jnp.arange(HEADS)[:, None] == lane_head[None, :]).astype(jnp.bfloat16)
    scale = jnp.dot(scale, spread, preferred_element_type=jnp.float32)
    payload = jnp.concatenate([q_payload, k_payload, v_payload])
    payload = jnp.pad(payload, ((0, 0), (0, (SLOTS - HEADS) * HEAD)))
    packed = (payload * scale.astype(jnp.bfloat16)).reshape(3 * ROWS, SLOTS, HEAD)
    return packed.transpose(1, 0, 2)


def exchange(array, groups):
    return lax.all_to_all(array, "device", 0, 0, axis_index_groups=groups.tolist(), tiled=True)


def body(q_payload, k_payload, v_payload, exponents, lengths):
    packed = pack(q_payload, k_payload, v_payload, exponents)
    mine = exchange(packed, BY_HEAD)
    query = mine[:, :ROWS].reshape(OWN, HEAD)
    own = mine[:, ROWS:].reshape(1, SLOTS, 2, ROWS, HEAD).transpose(0, 2, 1, 3, 4)
    own = own.reshape(1, 2, OWN, HEAD)
    near = exchange(jnp.concatenate([own] * 4), BY_X)
    far = lax.ppermute(near, "device", [(a, b) for a, b in BY_CORE.tolist()] + [(b, a) for a, b in BY_CORE.tolist()])
    state = attend(True, lengths, query, near)
    attended = attend(False, lengths, query, far, state)
    back = exchange(attended.reshape(SLOTS, ROWS, HEAD), BY_HEAD)
    return back[:HEADS].transpose(1, 0, 2).reshape(ROWS, HEADS * HEAD)


def solution(mesh):
    tokens = P("device", None)
    return jax.shard_map(
        body,
        mesh=Mesh(mesh.devices.reshape(-1), ("device",)),
        in_specs=(tokens, tokens, tokens, P(None, "device", None), P()),
        out_specs=tokens,
        check_vma=False,
    )
```

```python
import functools
import math

import jax
import jax.numpy as jnp
import numpy as np
from jax import lax
from jax.experimental import pallas as pl
from jax.experimental.pallas import tpu as pltpu
from jax.sharding import Mesh
from jax.sharding import PartitionSpec as P

SIZES = (8, 2, 2, 8, 2)
SLOTS = 64
HEADS = 48
HEAD = 128
ROWS = 8
OWN = SLOTS * ROWS
FIRST_Z, FIRST_Y = 5, 4
X_ORDER = [2, 1, 3, 0]
PLACES = np.arange(512).reshape(SIZES)
BY_HEAD = np.roll(PLACES, (-FIRST_Z, -FIRST_Y), (0, 3)).transpose(1, 2, 4, 3, 0).reshape(8, SLOTS)
BY_X = PLACES.transpose(0, 2, 3, 1, 4).reshape(128, 4)[:, X_ORDER]
BY_CORE = PLACES.transpose(0, 1, 3, 4, 2).reshape(256, 2)


def place():
    index = lax.axis_index("device")
    return (index // 32) % 2, index % 2, (index // 16) % 2


def clip_of(length_ref, token):
    first = length_ref[0]
    second = first + length_ref[1]
    third = second + length_ref[2]
    ends = (token >= first, token >= second, token >= third)
    return sum(end.astype(jnp.int32) for end in ends)


def token_of(row, xh, core, xl):
    z = ((row >> 3) + FIRST_Z) & 7
    y = ((row >> 6) + FIRST_Y) & 7
    return (z << 9) + (y << 4) + (row & 7) + (xh * 256 + core * 128 + xl * 8)


QB = 256


def attend_kernel(its_core, carried, length_ref, q_ref, kv_ref, *refs):
    if carried:
        acc_ref, top_ref, sum_ref, out_ref, s_ref = refs
    else:
        acc_ref, top_ref, sum_ref, s_ref = refs
    xh, xl, core = place()
    key_core = core if its_core else 1 - core
    factor = math.log2(math.e) / math.sqrt(HEAD)
    key_row = lax.broadcasted_iota(jnp.int32, (1, OWN), 1)
    key_clip = [
        clip_of(length_ref, token_of(key_row, x // 2, key_core, x % 2)) for x in X_ORDER
    ]
    blocks = OWN // QB

    def rows(block):
        return slice(block * QB, (block + 1) * QB)

    def begin(block):
        query_row = block * QB + lax.broadcasted_iota(jnp.int32, (QB, 1), 0)
        query_clip = clip_of(length_ref, token_of(query_row, xh, core, xl))
        top = top_ref[rows(block), :] if carried else jnp.full((QB, HEAD), -1e30, jnp.float32)
        return q_ref[rows(block), :], query_clip, top

    def score(block, x, query, query_clip, top):
        scores = lax.dot_general(
            query, kv_ref[x, 0], (((1,), (1,)), ((), ())), preferred_element_type=jnp.float32
        )
        scores = jnp.where(query_clip == key_clip[x], scores, -1e30)
        s_ref[block % 2, :, x * OWN : (x + 1) * OWN] = scores
        for j in range(0, OWN, HEAD):
            top = jnp.maximum(top, scores[:, j : j + HEAD])
        return top

    query, query_clip, top = begin(0)
    for x in range(4):
        top = score(0, x, query, query_clip, top)
    for block in range(blocks):
        highest = jnp.max(top, axis=1, keepdims=True)
        shift = highest * factor
        total = numerator = jnp.zeros((QB, HEAD), jnp.float32)
        if block + 1 < blocks:
            query, query_clip, top = begin(block + 1)
        for x in range(4):
            if block + 1 < blocks and not carried:
                top = score(block + 1, x, query, query_clip, top)
            weights = jnp.exp2(s_ref[block % 2, :, x * OWN : (x + 1) * OWN] * factor - shift)
            for j in range(0, OWN, HEAD):
                total = total + weights[:, j : j + HEAD]
            if block + 1 < blocks and carried:
                top = score(block + 1, x, query, query_clip, top)
            numerator = numerator + jnp.dot(
                weights.astype(jnp.bfloat16), kv_ref[x, 1], preferred_element_type=jnp.float32
            )
        if carried:
            old = jnp.exp2(top_ref[rows(block), :] * factor - shift)
            total = total + sum_ref[rows(block), :] * old
            numerator = numerator + acc_ref[rows(block), :] * old
            out_ref[rows(block), :] = (
                numerator / jnp.sum(total, axis=1, keepdims=True)
            ).astype(jnp.bfloat16)
        else:
            acc_ref[rows(block), :] = numerator
            top_ref[rows(block), :] = jnp.broadcast_to(highest, (QB, HEAD))
            sum_ref[rows(block), :] = total


VMEM = pl.BlockSpec(memory_space=pltpu.VMEM)
SMEM = pl.BlockSpec(memory_space=pltpu.SMEM)


def attend(its_core, lengths, query, kv, state=()):
    f32 = jax.ShapeDtypeStruct((OWN, HEAD), jnp.float32)
    return pl.pallas_call(
        functools.partial(attend_kernel, its_core, bool(state)),
        out_shape=jax.ShapeDtypeStruct((OWN, HEAD), jnp.bfloat16) if state else [f32] * 3,
        in_specs=[SMEM] + [VMEM] * (2 + len(state)),
        out_specs=VMEM if state else [VMEM] * 3,
        scratch_shapes=[pltpu.VMEM((2, QB, 4 * OWN), jnp.float32)],
        compiler_params=pltpu.CompilerParams(vmem_limit_bytes=32 * 2**20),
        cost_estimate=pl.CostEstimate(
            flops=4 * OWN * 4 * OWN * HEAD, bytes_accessed=2**20, transcendentals=4 * OWN * OWN
        ),
    )(lengths, query, kv, *state)


def pack(q_payload, k_payload, v_payload, exponents):
    scale = jnp.exp2(exponents.astype(jnp.float32)).astype(jnp.bfloat16).reshape(3 * ROWS, HEADS)
    lane_head = jnp.arange(SLOTS * HEAD) // HEAD
    spread = (jnp.arange(HEADS)[:, None] == lane_head[None, :]).astype(jnp.bfloat16)
    scale = jnp.dot(scale, spread, preferred_element_type=jnp.float32)
    payload = jnp.concatenate([q_payload, k_payload, v_payload])
    payload = jnp.pad(payload, ((0, 0), (0, (SLOTS - HEADS) * HEAD)))
    packed = (payload * scale.astype(jnp.bfloat16)).reshape(3 * ROWS, SLOTS, HEAD)
    return packed.transpose(1, 0, 2)


def exchange(array, groups):
    return lax.all_to_all(array, "device", 0, 0, axis_index_groups=groups.tolist(), tiled=True)


def body(q_payload, k_payload, v_payload, exponents, lengths):
    packed = pack(q_payload, k_payload, v_payload, exponents)
    mine = exchange(packed, BY_HEAD)
    query = mine[:, :ROWS].reshape(OWN, HEAD)
    own = mine[:, ROWS:].reshape(1, SLOTS, 2, ROWS, HEAD).transpose(0, 2, 1, 3, 4)
    own = own.reshape(1, 2, OWN, HEAD)
    near = exchange(jnp.concatenate([own] * 4), BY_X)
    far = lax.ppermute(near, "device", [(a, b) for a, b in BY_CORE.tolist()] + [(b, a) for a, b in BY_CORE.tolist()])
    state = attend(True, lengths, query, near)
    attended = attend(False, lengths, query, far, state)
    back = exchange(attended.reshape(SLOTS, ROWS, HEAD), BY_HEAD)
    return back[:HEADS].transpose(1, 0, 2).reshape(ROWS, HEADS * HEAD)


def solution(mesh):
    tokens = P("device", None)
    return jax.shard_map(
        body,
        mesh=Mesh(mesh.devices.reshape(-1), ("device",)),
        in_specs=(tokens, tokens, tokens, P(None, "device", None), P()),
        out_specs=tokens,
        check_vma=False,
    )
```

```python
import functools
import math

import jax
import jax.numpy as jnp
import numpy as np
from jax import lax
from jax.experimental import pallas as pl
from jax.experimental.pallas import tpu as pltpu
from jax.sharding import Mesh
from jax.sharding import PartitionSpec as P

SIZES = (8, 2, 2, 8, 2)
SLOTS = 64
HEADS = 48
HEAD = 128
ROWS = 8
OWN = SLOTS * ROWS
FIRST_Z, FIRST_Y = 6, 4
X_ORDER = [2, 1, 3, 0]
PLACES = np.arange(512).reshape(SIZES)
BY_HEAD = np.roll(PLACES, (-FIRST_Z, -FIRST_Y), (0, 3)).transpose(1, 2, 4, 3, 0).reshape(8, SLOTS)
BY_X = PLACES.transpose(0, 2, 3, 1, 4).reshape(128, 4)[:, X_ORDER]
BY_CORE = PLACES.transpose(0, 1, 3, 4, 2).reshape(256, 2)


def place():
    index = lax.axis_index("device")
    return (index // 32) % 2, index % 2, (index // 16) % 2


def clip_of(length_ref, token):
    first = length_ref[0]
    second = first + length_ref[1]
    third = second + length_ref[2]
    ends = (token >= first, token >= second, token >= third)
    return sum(end.astype(jnp.int32) for end in ends)


def token_of(row, xh, core, xl):
    z = ((row >> 3) + FIRST_Z) & 7
    y = ((row >> 6) + FIRST_Y) & 7
    return (z << 9) + (y << 4) + (row & 7) + (xh * 256 + core * 128 + xl * 8)


QB = 256


def attend_kernel(its_core, carried, length_ref, q_ref, kv_ref, *refs):
    if carried:
        acc_ref, top_ref, sum_ref, out_ref, s_ref = refs
    else:
        acc_ref, top_ref, sum_ref, s_ref = refs
    xh, xl, core = place()
    key_core = core if its_core else 1 - core
    factor = math.log2(math.e) / math.sqrt(HEAD)
    key_row = lax.broadcasted_iota(jnp.int32, (1, OWN), 1)
    key_clip = [
        clip_of(length_ref, token_of(key_row, x // 2, key_core, x % 2)) for x in X_ORDER
    ]
    blocks = OWN // QB

    def rows(block):
        return slice(block * QB, (block + 1) * QB)

    def begin(block):
        query_row = block * QB + lax.broadcasted_iota(jnp.int32, (QB, 1), 0)
        query_clip = clip_of(length_ref, token_of(query_row, xh, core, xl))
        top = top_ref[rows(block), :] if carried else jnp.full((QB, HEAD), -1e30, jnp.float32)
        return q_ref[rows(block), :], query_clip, top

    def score(block, x, query, query_clip, top):
        scores = lax.dot_general(
            query, kv_ref[x, 0], (((1,), (1,)), ((), ())), preferred_element_type=jnp.float32
        )
        scores = jnp.where(query_clip == key_clip[x], scores, -1e30)
        s_ref[block % 2, :, x * OWN : (x + 1) * OWN] = scores
        for j in range(0, OWN, HEAD):
            top = jnp.maximum(top, scores[:, j : j + HEAD])
        return top

    query, query_clip, top = begin(0)
    for x in range(4):
        top = score(0, x, query, query_clip, top)
    for block in range(blocks):
        highest = jnp.max(top, axis=1, keepdims=True)
        shift = highest * factor
        total = numerator = jnp.zeros((QB, HEAD), jnp.float32)
        if block + 1 < blocks:
            query, query_clip, top = begin(block + 1)
        for x in range(4):
            if block + 1 < blocks:
                top = score(block + 1, x, query, query_clip, top)
            weights = jnp.exp2(s_ref[block % 2, :, x * OWN : (x + 1) * OWN] * factor - shift)
            for j in range(0, OWN, HEAD):
                total = total + weights[:, j : j + HEAD]
            numerator = numerator + jnp.dot(
                weights.astype(jnp.bfloat16), kv_ref[x, 1], preferred_element_type=jnp.float32
            )
        if carried:
            old = jnp.exp2(top_ref[rows(block), :] * factor - shift)
            total = total + sum_ref[rows(block), :] * old
            numerator = numerator + acc_ref[rows(block), :] * old
            out_ref[rows(block), :] = (
                numerator / jnp.sum(total, axis=1, keepdims=True)
            ).astype(jnp.bfloat16)
        else:
            acc_ref[rows(block), :] = numerator
            top_ref[rows(block), :] = jnp.broadcast_to(highest, (QB, HEAD))
            sum_ref[rows(block), :] = total


VMEM = pl.BlockSpec(memory_space=pltpu.VMEM)
SMEM = pl.BlockSpec(memory_space=pltpu.SMEM)


def attend(its_core, lengths, query, kv, state=()):
    f32 = jax.ShapeDtypeStruct((OWN, HEAD), jnp.float32)
    return pl.pallas_call(
        functools.partial(attend_kernel, its_core, bool(state)),
        out_shape=jax.ShapeDtypeStruct((OWN, HEAD), jnp.bfloat16) if state else [f32] * 3,
        in_specs=[SMEM] + [VMEM] * (2 + len(state)),
        out_specs=VMEM if state else [VMEM] * 3,
        scratch_shapes=[pltpu.VMEM((2, QB, 4 * OWN), jnp.float32)],
        compiler_params=pltpu.CompilerParams(vmem_limit_bytes=32 * 2**20),
        cost_estimate=pl.CostEstimate(
            flops=4 * OWN * 4 * OWN * HEAD, bytes_accessed=2**20, transcendentals=4 * OWN * OWN
        ),
    )(lengths, query, kv, *state)


def pack(q_payload, k_payload, v_payload, exponents):
    scale = jnp.exp2(exponents.astype(jnp.float32)).astype(jnp.bfloat16).reshape(3 * ROWS, HEADS)
    lane_head = jnp.arange(SLOTS * HEAD) // HEAD
    spread = (jnp.arange(HEADS)[:, None] == lane_head[None, :]).astype(jnp.bfloat16)
    scale = jnp.dot(scale, spread, preferred_element_type=jnp.float32)
    payload = jnp.concatenate([q_payload, k_payload, v_payload])
    payload = jnp.pad(payload, ((0, 0), (0, (SLOTS - HEADS) * HEAD)))
    packed = (payload * scale.astype(jnp.bfloat16)).reshape(3 * ROWS, SLOTS, HEAD)
    return packed.transpose(1, 0, 2)


def exchange(array, groups):
    return lax.all_to_all(array, "device", 0, 0, axis_index_groups=groups.tolist(), tiled=True)


def body(q_payload, k_payload, v_payload, exponents, lengths):
    packed = pack(q_payload, k_payload, v_payload, exponents)
    mine = exchange(packed, BY_HEAD)
    query = mine[:, :ROWS].reshape(OWN, HEAD)
    own = mine[:, ROWS:].reshape(1, SLOTS, 2, ROWS, HEAD).transpose(0, 2, 1, 3, 4)
    own = own.reshape(1, 2, OWN, HEAD)
    near = exchange(jnp.concatenate([own] * 4), BY_X)
    far = lax.ppermute(near, "device", [(a, b) for a, b in BY_CORE.tolist()] + [(b, a) for a, b in BY_CORE.tolist()])
    state = attend(True, lengths, query, near)
    attended = attend(False, lengths, query, far, state)
    back = exchange(attended.reshape(SLOTS, ROWS, HEAD), BY_HEAD)
    return back[:HEADS].transpose(1, 0, 2).reshape(ROWS, HEADS * HEAD)


def solution(mesh):
    tokens = P("device", None)
    return jax.shard_map(
        body,
        mesh=Mesh(mesh.devices.reshape(-1), ("device",)),
        in_specs=(tokens, tokens, tokens, P(None, "device", None), P()),
        out_specs=tokens,
        check_vma=False,
    )
```
